32 devices in a mesh: seq: 8 (over z, x), ch: 4 (over y, core).
Axes of the slice: x: 2, y: 2, z: 4, core: 2. Of those that a mesh axis runs over, the one named last changes fastest.
Arguments:
- block_input: bfloat16 [8192, 2048], P('ch', 'seq'), may hold values from -110 to 110
- norm_gain: float32 [8192], P('ch'), may hold values from 0.1 to 1.9
- short_taps: bfloat16 [8192, 7], P('ch'), may hold values from -2 to 2
- medium_taps: bfloat16 [8192, 128], P('ch'), may hold values from -0.5 to 0.5
- long_filter: float32 [8192, 2048], P(('ch', 'seq')), may hold values from -2 to 2
- grad_out: bfloat16 [8192, 2048], P('ch', 'seq'), may hold values from -2.390625 to 2.390625
Outputs:
- grad_normed: bfloat16 [8192, 2048], P('ch', 'seq')
- grad_long: float32 [8192, 2048], P(('ch', 'seq'))
- grad_medium: float32 [8192, 128], P(('ch', 'seq'))
- grad_short: float32 [8192, 7], P(('ch', 'seq'))
The draws below stay inside these ranges and needn't reach their ends.
All inputs are finite; a program needn't handle non-finite values.
Results may differ from the reference program's by a relative error of at most 0.0058.
Values may be sent and summed in bfloat16 or wider, within the bound.
A program may use at most 128 MiB of HBM per device.

```python
import math
import jax
import jax.numpy as jnp
from jax import lax

D = 8192
SHORT = 7
MED = 128
SEQ = 2048


def draw_block_input(key, part):
    key_col, key_row, key_val = jax.random.split(key, 3)
    channel = jnp.arange(D, dtype=jnp.float32) / D
    column = jnp.exp(jax.random.uniform(key_col, (D, 1), jnp.float32, 0.0, math.log(10.0)))
    row = jnp.exp(jax.random.uniform(key_row, (1, SEQ), jnp.float32, 0.0, math.log(10.0)))
    rise = jnp.exp(channel * 0.5 * math.log(3.0))[:, None]
    value = jnp.clip(jax.random.normal(key_val, (D, SEQ), jnp.float32), -6.0, 6.0)
    return (0.1 * value * column * row * rise).astype(jnp.bfloat16)


def draw_long_filter(key, part):
    key_kind, key_slow, key_fast, key_val = jax.random.split(key, 4)
    position = jnp.arange(SEQ, dtype=jnp.float32)[None, :]
    share = 0.5
    slow = jax.random.uniform(key_kind, (D, 1), jnp.float32) < share
    slow_rate = jnp.exp(jax.random.uniform(key_slow, (D, 1), jnp.float32, math.log(0.1 / SEQ), math.log(2.0 / SEQ)))
    fast_rate = jnp.exp(jax.random.uniform(key_fast, (D, 1), jnp.float32, math.log(1.0 / 50.0), math.log(1.0 / 30.0)))
    rate = jnp.where(slow, slow_rate, fast_rate)
    norm_factor = jnp.sqrt(jnp.expm1(-2.0 * rate) / jnp.expm1(-2.0 * rate * SEQ))
    value = jnp.clip(jax.random.normal(key_val, (D, SEQ), jnp.float32), -6.0, 6.0)
    return (value * jnp.exp(-rate * position) * norm_factor).astype(jnp.float32)


def shard_levels(stream_key, dims, shards, smallest, high):
    loudness, own = 1.0, jax.random.fold_in(stream_key, 6)
    for axis_at, shards_of in shards:
        draws = jnp.exp(jax.random.uniform(jax.random.fold_in(own, axis_at), (shards_of,), jnp.float32, smallest / len(shards), high / len(shards)))
        loudness = loudness * jnp.repeat(draws, dims[axis_at] // shards_of).reshape([-1 if axis == axis_at else 1 for axis in range(len(dims))])
    return loudness


def gaussian(rng, shape, deviation, most, cuts=(), held_as=jnp.bfloat16):
    result = deviation * jax.random.normal(rng, shape, jnp.float32)
    if cuts:
        result = result * shard_levels(rng, shape, cuts, -0.22, 0.18)
    return jnp.clip(result, -most, most).astype(held_as)


def setup_inputs(seed: int = 0) -> dict:
    key_of = jax.random.split(jax.random.key(seed), 7)
    return {
        "block_input": draw_block_input(jax.random.fold_in(key_of[6], 71), 0),
        "norm_gain": jnp.clip(1.0 + 0.18 * jax.random.normal(key_of[1], (D,), jnp.float32), 0.1, 1.9),
        "short_taps": gaussian(key_of[2], (D, SHORT), SHORT ** -0.5, 2.0, ((0, 4),)),
        "medium_taps": gaussian(key_of[3], (D, MED), MED ** -0.5, 0.5, ((0, 4),)),
        "long_filter": draw_long_filter(jax.random.fold_in(key_of[6], 71), 0),
        "grad_out": gaussian(key_of[5], (D, SEQ), 0.4, 2.390625, ((0, 4), (1, 8))),
    }


def causal_sum(signal, taps):
    count = taps.shape[1]
    width = signal.shape[1]
    padded = jnp.pad(signal.astype(jnp.float32), ((0, 0), (count - 1, 0)))
    weights = taps.astype(jnp.float32)

    def add_lag(lag, total):
        lag_index = jnp.asarray(lag).astype(jnp.int32)
        piece = lax.dynamic_slice_in_dim(padded, (count - 1 - lag_index).astype(jnp.int32), width, 1)
        column = lax.dynamic_slice_in_dim(weights, lag_index, 1, 1)
        return total + column * piece
    return lax.fori_loop(0, count, add_lag, jnp.zeros(signal.shape, jnp.float32))

def ahead_sum(signal, taps):
    count = taps.shape[1]
    width = signal.shape[1]
    padded = jnp.pad(signal.astype(jnp.float32), ((0, 0), (0, count - 1)))
    weights = taps.astype(jnp.float32)

    def add_lag(lag, total):
        lag_index = jnp.asarray(lag).astype(jnp.int32)
        piece = lax.dynamic_slice_in_dim(padded, lag_index, width, 1)
        column = lax.dynamic_slice_in_dim(weights, lag_index, 1, 1)
        return total + column * piece
    return lax.fori_loop(0, count, add_lag, jnp.zeros(signal.shape, jnp.float32))

def lag_products(grad, signal, count):
    width = signal.shape[1]
    padded = jnp.pad(signal.astype(jnp.float32), ((0, 0), (count - 1, 0)))
    grad32 = grad.astype(jnp.float32)

    def one_lag(lag):
        piece = lax.dynamic_slice_in_dim(padded, (count - 1 - lag).astype(jnp.int32), width, 1)
        return lax.optimization_barrier(jnp.sum(grad32 * piece, axis=1))
    return lax.map(one_lag, jnp.arange(count, dtype=jnp.int32)).T

def reference(block_input, norm_gain, short_taps, medium_taps, long_filter, grad_out):
    inputs32 = block_input.astype(jnp.float32)
    inv_rms = lax.rsqrt(lax.optimization_barrier(jnp.mean(inputs32 * inputs32, axis=0)) + 1e-05)
    normed = (inputs32 * inv_rms[None, :] * norm_gain[:, None]).astype(jnp.bfloat16)
    shorted = causal_sum(normed, short_taps).astype(jnp.bfloat16)
    filtered = causal_sum(shorted, medium_taps).astype(jnp.bfloat16)
    block = math.gcd(D, 256)
    groups = D // block
    total = 2 * SEQ

    def long_part(pieces):
        filt_piece, grad_piece, sig_piece = pieces
        filt_hat = jnp.fft.rfft(filt_piece.astype(jnp.float32), n=total, axis=1)
        grad_hat = jnp.fft.rfft(grad_piece.astype(jnp.float32), n=total, axis=1)
        sig_hat = jnp.fft.rfft(sig_piece.astype(jnp.float32), n=total, axis=1)
        back_grad = jnp.fft.irfft(jnp.conj(filt_hat) * grad_hat, n=total, axis=1)[:, :SEQ]
        back_filt = jnp.fft.irfft(jnp.conj(sig_hat) * grad_hat, n=total, axis=1)[:, :SEQ]
        return (back_grad.astype(jnp.bfloat16), back_filt.astype(jnp.float32))
    grad_filtered, long_raw = lax.map(long_part, (long_filter.reshape(groups, block, SEQ), grad_out.reshape(groups, block, SEQ), filtered.reshape(groups, block, SEQ)))
    grad_filtered = grad_filtered.reshape(D, SEQ)
    scale = SEQ ** (-0.5)
    grad_long = long_raw.reshape(D, SEQ) * scale
    grad_shorted = ahead_sum(grad_filtered, medium_taps).astype(jnp.bfloat16)
    grad_normed = ahead_sum(grad_shorted, short_taps).astype(jnp.bfloat16)
    grad_medium = lag_products(grad_filtered, shorted, MED) * scale
    grad_short = lag_products(grad_shorted, normed, SHORT) * scale
    return (grad_normed, grad_long, grad_medium, grad_short)
```

```python
import functools
import math

import jax
import jax.numpy as jnp
import ml_dtypes
import numpy as np
from jax import lax
from jax.experimental import pallas as pl
from jax.experimental.pallas import tpu as pltpu
from jax.sharding import PartitionSpec as P

LANES = 128
ROWS = 16
CHUNKS = 1


def halves(table):
    high = table.astype(np.float32).astype(ml_dtypes.bfloat16)
    low = (table - high.astype(np.float64)).astype(np.float32).astype(ml_dtypes.bfloat16)
    return high, low


@functools.lru_cache(maxsize=None)
def tables(blocks):
    outer = blocks + 1
    k = np.arange(outer)[:, None]
    a = np.arange(blocks)[None, :]
    q = np.arange(LANES)
    angle = 2.0 * math.pi * ((4 * k + 1) * a % (4 * outer)) / (4.0 * outer)
    eye = np.eye(ROWS)
    split = np.stack([np.cos(angle), -np.sin(angle)])
    ahead = np.einsum("xka,cd->xkcad", split, eye)
    ahead = ahead.reshape(2 * outer * ROWS, blocks * ROWS)
    back = ahead.T
    twist = 2.0 * math.pi * (4 * k + 1) * q[None, :] / (4.0 * outer * LANES)
    twist_re = np.repeat(np.cos(twist), ROWS, axis=0).astype(np.float32)
    twist_im = np.repeat(-np.sin(twist), ROWS, axis=0).astype(np.float32)
    inner = 2.0 * math.pi * (q[:, None] * q[None, :] % LANES) / LANES
    cos, sin = np.cos(inner), np.sin(inner)
    turn = np.block([[cos, -sin], [sin, cos]])
    return (
        *halves(ahead),
        *halves(back),
        twist_re,
        twist_im,
        *halves(turn),
        *halves(turn.T),
    )


def times(a, b):
    return (a[0] * b[0] - a[1] * b[1], a[0] * b[1] + a[1] * b[0])


def times_conj(a, b):
    return (a[0] * b[0] + a[1] * b[1], a[1] * b[0] - a[0] * b[1])


def dot(a, b):
    return jnp.dot(a, b, preferred_element_type=jnp.float32)


def parted(value):
    high = value.astype(jnp.bfloat16)
    return high, (value - high.astype(jnp.float32)).astype(jnp.bfloat16)


def spectral_kernel(
    blocks,
    x_ref,
    g_ref,
    h_ref,
    inv_ref,
    gain_ref,
    short_ref,
    medium_ref,
    ahead_hi,
    ahead_lo,
    back_hi,
    back_lo,
    twist_re,
    twist_im,
    turn_hi,
    turn_lo,
    turn_back_hi,
    turn_back_lo,
    normed_out,
    long_out,
    medium_out,
    short_out,
    first,
    last_hi,
    last_lo,
):
    outer = blocks + 1
    groups = x_ref.shape[1] // ROWS
    per = x_ref.shape[2] // LANES
    half = outer * ROWS
    scale = 1.0 / (outer * LANES)
    root = (blocks * LANES) ** (-0.5)

    def piece(ref, group, block):
        lanes = slice((block % per) * LANES, (block % per + 1) * LANES)
        return ref[block // per, group * ROWS : (group + 1) * ROWS, lanes]

    def normed_piece(group, block):
        raw = piece(x_ref, group, block).astype(jnp.float32)
        inv = inv_ref[:, block * LANES : (block + 1) * LANES]
        gain = gain_ref[group * ROWS : (group + 1) * ROWS, :]
        return (raw * inv * gain).astype(jnp.bfloat16)

    for group in range(groups):
        lanes = slice(group * LANES, (group + 1) * LANES)
        rows = slice(group * ROWS, (group + 1) * ROWS)
        normed = jnp.concatenate([normed_piece(group, b) for b in range(blocks)], axis=0)
        grads = jnp.concatenate([piece(g_ref, group, b) for b in range(blocks)], axis=0)
        taps = jnp.concatenate(
            [h_ref[rows, b * LANES : (b + 1) * LANES] for b in range(blocks)], axis=0
        )
        taps_hi, taps_lo = parted(taps)
        pair = jnp.concatenate([normed, grads], axis=1)
        both = dot(ahead_hi[...], pair) + dot(ahead_lo[...], pair)
        first[0, :, lanes] = both[:, :LANES]
        first[1, :, lanes] = both[:, LANES:]
        pair = jnp.concatenate([taps_hi, taps_lo], axis=1)
        both = dot(ahead_hi[...], pair)
        first[2, :, lanes] = both[:, :LANES] + both[:, LANES:] + dot(ahead_lo[...], taps_hi)

    def at_freq(k, sums):
        top = pl.multiple_of(k * ROWS, ROWS)
        bottom = pl.multiple_of(half + k * ROWS, ROWS)
        t_re = twist_re[pl.ds(top, ROWS), :]
        t_im = twist_im[pl.ds(top, ROWS), :]
        stack = []
        for signal in range(3):
            for group in range(groups):
                lanes = slice(group * LANES, (group + 1) * LANES)
                value = (
                    first[signal, pl.ds(top, ROWS), lanes],
                    first[signal, pl.ds(bottom, ROWS), lanes],
                )
                stack.append(jnp.concatenate(times(value, (t_re, t_im)), axis=1))
        for ref in (short_ref, medium_ref):
            for group in range(groups):
                taps = ref[group * ROWS : (group + 1) * ROWS, :].astype(jnp.float32)
                stack.append(jnp.concatenate([taps * t_re, taps * t_im], axis=1))
        high, low = parted(jnp.concatenate(stack, axis=0))
        spec = dot(high, turn_hi[...]) + dot(low, turn_hi[...]) + dot(high, turn_lo[...])
        count = groups * ROWS
        normed, grads, taps, short, medium = [
            (spec[i * count : (i + 1) * count, :LANES], spec[i * count : (i + 1) * count, LANES:])
            for i in range(5)
        ]
        shorted = times(short, normed)
        grad_long = times_conj(grads, times(medium, shorted))
        grad_filtered = times_conj(grads, taps)
        grad_medium = times_conj(grad_filtered, shorted)
        grad_shorted = times_conj(grad_filtered, medium)
        grad_short = times_conj(grad_shorted, normed)
        grad_normed = times_conj(grad_shorted, short)
        stack = [
            jnp.concatenate(value, axis=1)
            for value in (grad_normed, grad_long, grad_medium, grad_short)
        ]
        high, low = parted(jnp.concatenate(stack, axis=0))
        step = (
            dot(high, turn_back_hi[...])
            + dot(low, turn_back_hi[...])
            + dot(high, turn_back_lo[...])
        )
        for signal in range(2):
            for group in range(groups):
                at = signal * count + group * ROWS
                lanes = slice(group * LANES, (group + 1) * LANES)
                value = (step[at : at + ROWS, :LANES], step[at : at + ROWS, LANES:])
                turned = times_conj(value, (t_re, t_im))
                for where, part in zip((top, bottom), turned):
                    part_hi, part_lo = parted(part)
                    last_hi[signal, pl.ds(where, ROWS), lanes] = part_hi
                    last_lo[signal, pl.ds(where, ROWS), lanes] = part_lo
        result = []
        for signal in range(2):
            for group in range(groups):
                at = (2 + signal) * count + group * ROWS
                real = step[at : at + ROWS, :LANES] * t_re + step[at : at + ROWS, LANES:] * t_im
                result.append(sums[signal * groups + group] + real)
        return tuple(result)

    zero = jnp.zeros((ROWS, LANES), jnp.float32)
    sums = lax.fori_loop(0, outer, at_freq, (zero,) * (2 * groups))
    for group in range(groups):
        rows = slice(group * ROWS, (group + 1) * ROWS)
        medium_out[rows, :] = sums[group] * (scale * root)
        short_out[rows, :] = sums[groups + group] * (scale * root)
    for signal in range(2):
        value = (
            dot(back_hi[...], last_hi[signal])
            + dot(back_hi[...], last_lo[signal])
            + dot(back_lo[...], last_hi[signal])
        )
        for group in range(groups):
            rows = slice(group * ROWS, (group + 1) * ROWS)
            for block in range(blocks):
                part = value[
                    block * ROWS : (block + 1) * ROWS, group * LANES : (group + 1) * LANES
                ]
                lanes = slice((block % per) * LANES, (block % per + 1) * LANES)
                if signal == 0:
                    normed_out[block // per, rows, lanes] = (part * scale).astype(jnp.bfloat16)
                else:
                    long_out[rows, block * LANES : (block + 1) * LANES] = part * (scale * root)


def spectral(x, g, h, inv, gain, short, medium, interpret=False):
    owners, chans, tokens = x.shape
    length = owners * tokens
    blocks = length // LANES
    outer = blocks + 1
    size = min(chans, 64 if blocks <= 16 else ROWS)
    consts = [jnp.asarray(t) for t in tables(blocks)]
    whole = pl.BlockSpec(memory_space=pltpu.VMEM)
    cut = pl.BlockSpec((owners, size, tokens), lambda i: (0, i, 0))

    def rows(width):
        return pl.BlockSpec((size, width), lambda i: (i, 0))

    lanes = size // ROWS * LANES
    return pl.pallas_call(
        functools.partial(spectral_kernel, blocks),
        grid=(chans // size,),
        in_specs=[
            cut,
            cut,
            rows(length),
            pl.BlockSpec((1, length), lambda i: (0, 0)),
            rows(1),
            rows(LANES),
            rows(LANES),
        ]
        + [whole] * len(consts),
        out_specs=[cut, rows(length), rows(LANES), rows(LANES)],
        out_shape=[
            jax.ShapeDtypeStruct((owners, chans, tokens), jnp.bfloat16),
            jax.ShapeDtypeStruct((chans, length), jnp.float32),
            jax.ShapeDtypeStruct((chans, LANES), jnp.float32),
            jax.ShapeDtypeStruct((chans, LANES), jnp.float32),
        ],
        scratch_shapes=[
            pltpu.VMEM((3, 2 * outer * ROWS, lanes), jnp.float32),
            pltpu.VMEM((2, 2 * outer * ROWS, lanes), jnp.bfloat16),
            pltpu.VMEM((2, 2 * outer * ROWS, lanes), jnp.bfloat16),
        ],
        compiler_params=pltpu.CompilerParams(vmem_limit_bytes=56 * 1024 * 1024),
        interpret=interpret,
    )(x, g, h, inv, gain, short, medium, *consts)


def on_device(block_input, norm_gain, short_taps, medium_taps, long_filter, grad_out, interpret=False):
    chans, tokens = block_input.shape
    seq_count = lax.axis_size("seq")
    ch_count = lax.axis_size("ch")
    group = chans // seq_count
    length = seq_count * tokens
    short_count = short_taps.shape[1]
    inputs32 = block_input.astype(jnp.float32)
    squares = jnp.sum(inputs32 * inputs32, axis=0)
    everyones = lax.all_gather(squares, ("ch", "seq")).reshape(ch_count, length)
    inv_rms = lax.rsqrt(jnp.sum(everyones, axis=0) / (chans * ch_count) + 1e-05)[None, :]
    offset = lax.axis_index("seq") * group
    gain = lax.dynamic_slice_in_dim(norm_gain, offset, group, 0)[:, None]
    short = lax.dynamic_slice_in_dim(short_taps, offset, group, 0)
    short = jnp.pad(short, ((0, 0), (0, LANES - short_count)))
    medium = lax.dynamic_slice_in_dim(medium_taps, offset, group, 0)
    chunks = CHUNKS if group % (CHUNKS * ROWS) == 0 else 1
    part = group // chunks
    x_all = block_input.reshape(seq_count, group, tokens)
    g_all = grad_out.reshape(seq_count, group, tokens)
    results = []
    for chunk in range(chunks):
        at = slice(chunk * part, (chunk + 1) * part)
        x = lax.all_to_all(x_all[:, at], "seq", split_axis=0, concat_axis=0, tiled=True)
        g = lax.all_to_all(g_all[:, at], "seq", split_axis=0, concat_axis=0, tiled=True)
        normed, long, med, sho = spectral(
            x, g, long_filter[at], inv_rms, gain[at], short[at], medium[at], interpret
        )
        normed = lax.all_to_all(normed, "seq", split_axis=0, concat_axis=0, tiled=True)
        results.append((normed, long, med, sho[:, :short_count]))
    if chunks == 1:
        normed, long, med, sho = results[0]
    else:
        normed = jnp.concatenate([r[0] for r in results], axis=1)
        long, med, sho = [jnp.concatenate([r[i] for r in results], axis=0) for i in (1, 2, 3)]
    return (normed.reshape(chans, tokens), long, med[:, : medium_taps.shape[1]], sho)


def solution(mesh):
    placed = (
        P("ch", "seq"),
        P("ch"),
        P("ch", None),
        P("ch", None),
        P(("ch", "seq"), None),
        P("ch", "seq"),
    )
    return jax.shard_map(
        on_device,
        mesh=mesh,
        in_specs=placed,
        out_specs=(
            P("ch", "seq"),
            P(("ch", "seq"), None),
            P(("ch", "seq"), None),
            P(("ch", "seq"), None),
        ),
        check_vma=False,
    )
```

```python
import functools
import math

import jax
import jax.numpy as jnp
import ml_dtypes
import numpy as np
from jax import lax
from jax.experimental import pallas as pl
from jax.experimental.pallas import tpu as pltpu
from jax.sharding import PartitionSpec as P

LANES = 128
ROWS = 16
SIZE = 64


def halves(table):
    high = table.astype(np.float32).astype(ml_dtypes.bfloat16)
    low = (table - high.astype(np.float64)).astype(np.float32).astype(ml_dtypes.bfloat16)
    return high, low


@functools.lru_cache(maxsize=None)
def tables(blocks):
    outer = blocks + 1
    k = np.arange(outer)[:, None]
    a = np.arange(blocks)[None, :]
    q = np.arange(LANES)
    angle = 2.0 * math.pi * ((4 * k + 1) * a % (4 * outer)) / (4.0 * outer)
    eye = np.eye(ROWS)
    split = np.stack([np.cos(angle), -np.sin(angle)])
    ahead = np.einsum("xka,cd->xkcad", split, eye)
    ahead = ahead.reshape(2 * outer * ROWS, blocks * ROWS)
    back = ahead.T
    twist = 2.0 * math.pi * (4 * k + 1) * q[None, :] / (4.0 * outer * LANES)
    twist_re = np.repeat(np.cos(twist), ROWS, axis=0).astype(np.float32)
    twist_im = np.repeat(-np.sin(twist), ROWS, axis=0).astype(np.float32)
    inner = 2.0 * math.pi * (q[:, None] * q[None, :] % LANES) / LANES
    cos, sin = np.cos(inner), np.sin(inner)
    turn = np.block([[cos, -sin], [sin, cos]])
    return (
        *halves(ahead),
        *halves(back),
        twist_re,
        twist_im,
        *halves(turn),
        *halves(turn.T),
    )


def times(a, b):
    return (a[0] * b[0] - a[1] * b[1], a[0] * b[1] + a[1] * b[0])


def times_conj(a, b):
    return (a[0] * b[0] + a[1] * b[1], a[1] * b[0] - a[0] * b[1])


def dot(a, b):
    return jnp.dot(a, b, preferred_element_type=jnp.float32)


def parted(value):
    high = value.astype(jnp.bfloat16)
    return high, (value - high.astype(jnp.float32)).astype(jnp.bfloat16)


def fused_kernel(
    blocks,
    size,
    chunks,
    total_chans,
    x_ref,
    g_ref,
    h_ref,
    gain_ref,
    short_ref,
    medium_ref,
    ahead_hi,
    ahead_lo,
    back_hi,
    back_lo,
    twist_re,
    twist_im,
    turn_hi,
    turn_lo,
    turn_back_hi,
    turn_back_lo,
    normed_out,
    long_out,
    medium_out,
    short_out,
    normed_ref,
    x_in,
    g_in,
    leaving,
    squares,
    first,
    last_hi,
    last_lo,
    send_sem,
    recv_sem,
    square_send,
    square_recv,
):
    seq_count, group_chans, tokens = x_in.shape
    ch_count = squares.shape[0]
    me = lax.axis_index("seq")
    my_ch = lax.axis_index("ch")
    outer = blocks + 1
    groups = size // ROWS
    per = tokens // LANES
    half = outer * ROWS
    scale = 1.0 / (outer * LANES)
    root = (blocks * LANES) ** (-0.5)

    barrier = pltpu.get_barrier_semaphore()
    for d in range(1, seq_count):
        pl.semaphore_signal(
            barrier,
            inc=1,
            device_id={"seq": lax.rem(me + d, seq_count)},
            device_id_type=pl.DeviceIdType.MESH,
        )
    for d in range(1, ch_count):
        pl.semaphore_signal(
            barrier,
            inc=1,
            device_id={"ch": lax.rem(my_ch + d, ch_count)},
            device_id_type=pl.DeviceIdType.MESH,
        )
    pl.semaphore_wait(barrier, seq_count + ch_count - 2)

    def aligned(row):
        return pl.multiple_of(row, ROWS)

    def inward(which, chunk, d):
        to = lax.rem(me + d, seq_count)
        source = (g_ref, normed_ref)[which]
        target = (g_in, x_in)[which]
        return pltpu.make_async_remote_copy(
            src_ref=source.at[pl.ds(aligned(to * group_chans + chunk * size), size)],
            dst_ref=target.at[me, pl.ds(aligned(chunk * size), size)],
            send_sem=send_sem.at[which, chunk, d],
            recv_sem=recv_sem.at[which, chunk, d],
            device_id={"seq": to},
            device_id_type=pl.DeviceIdType.MESH,
        )

    def outward(chunk, d):
        to = lax.rem(me + d, seq_count)
        return pltpu.make_async_remote_copy(
            src_ref=leaving.at[to, pl.ds(aligned(chunk * size), size)],
            dst_ref=normed_out.at[pl.ds(aligned(me * group_chans + chunk * size), size)],
            send_sem=send_sem.at[2, chunk, d],
            recv_sem=recv_sem.at[2, chunk, d],
            device_id={"seq": to},
            device_id_type=pl.DeviceIdType.MESH,
        )

    def square_copy(d):
        return pltpu.make_async_remote_copy(
            src_ref=squares.at[my_ch],
            dst_ref=squares.at[my_ch],
            send_sem=square_send.at[d],
            recv_sem=square_recv.at[d],
            device_id={"ch": lax.rem(my_ch + d, ch_count)},
            device_id_type=pl.DeviceIdType.MESH,
        )

    def each_partner(act):
        lax.fori_loop(1, seq_count, lambda d, none: act(d), None)

    each_partner(lambda d: inward(0, 0, d).start())
    my_rows = pl.ds(aligned(me * group_chans), group_chans)
    g_in[me] = g_ref[my_rows, :]

    step = 8 * ROWS

    def add_rows(i, total):
        value = x_ref[pl.ds(aligned(i * step), step), :].astype(jnp.float32)
        return total + jnp.sum((value * value).reshape(step // 8, 8, tokens), axis=0)

    squares[my_ch] = lax.fori_loop(
        0, x_ref.shape[0] // step, add_rows, jnp.zeros((8, tokens), jnp.float32)
    )
    for d in range(1, ch_count):
        square_copy(d).start()
    for d in range(1, ch_count):
        square_copy(d).wait()
    mean = jnp.sum(jnp.sum(squares[...], axis=0), axis=0, keepdims=True) / total_chans
    inv_rms = lax.rsqrt(mean + 1e-05)

    def prepare(chunk, none):
        def one(d, none):
            to = lax.rem(me + d, seq_count)
            at = pl.ds(aligned(to * group_chans + chunk * size), size)
            value = x_ref[at, :].astype(jnp.float32) * inv_rms * gain_ref[at, :]
            normed_ref[at, :] = value.astype(jnp.bfloat16)

            @pl.when(d > 0)
            def _():
                inward(1, chunk, d).start()

        lax.fori_loop(0, seq_count, one, None)

        @pl.when(chunk + 1 < chunks)
        def _():
            each_partner(lambda d: inward(0, chunk + 1, d).start())

    lax.fori_loop(0, chunks, prepare, None)
    x_in[me] = normed_ref[my_rows, :]

    def work(chunk, none):
        def arrive(d):
            inward(0, chunk, d).wait_recv()
            inward(1, chunk, d).wait_recv()

        each_partner(arrive)
        local = chunk * size
        mine = me * group_chans + local

        def rows_at(start, group):
            return pl.ds(aligned(start + group * ROWS), ROWS)

        def piece(ref, group, block):
            lanes = slice((block % per) * LANES, (block % per + 1) * LANES)
            return ref[block // per, rows_at(local, group), lanes]

        for group in range(groups):
            lanes = slice(group * LANES, (group + 1) * LANES)
            rows = rows_at(local, group)
            normed = jnp.concatenate([piece(x_in, group, b) for b in range(blocks)], axis=0)
            grads = jnp.concatenate([piece(g_in, group, b) for b in range(blocks)], axis=0)
            taps = jnp.concatenate(
                [h_ref[rows, b * LANES : (b + 1) * LANES] for b in range(blocks)], axis=0
            )
            taps_hi, taps_lo = parted(taps)
            pair = jnp.concatenate([normed, grads], axis=1)
            both = dot(ahead_hi[...], pair) + dot(ahead_lo[...], pair)
            first[0, :, lanes] = both[:, :LANES]
            first[1, :, lanes] = both[:, LANES:]
            pair = jnp.concatenate([taps_hi, taps_lo], axis=1)
            both = dot(ahead_hi[...], pair)
            first[2, :, lanes] = both[:, :LANES] + both[:, LANES:] + dot(ahead_lo[...], taps_hi)

        def at_freq(k, sums):
            top = pl.multiple_of(k * ROWS, ROWS)
            bottom = pl.multiple_of(half + k * ROWS, ROWS)
            t_re = twist_re[pl.ds(top, ROWS), :]
            t_im = twist_im[pl.ds(top, ROWS), :]
            stack = []
            for signal in range(3):
                for group in range(groups):
                    lanes = slice(group * LANES, (group + 1) * LANES)
                    value = (
                        first[signal, pl.ds(top, ROWS), lanes],
                        first[signal, pl.ds(bottom, ROWS), lanes],
                    )
                    stack.append(jnp.concatenate(times(value, (t_re, t_im)), axis=1))
            for ref, start in ((short_ref, local), (medium_ref, mine)):
                for group in range(groups):
                    taps = ref[rows_at(start, group), :].astype(jnp.float32)
                    stack.append(jnp.concatenate([taps * t_re, taps * t_im], axis=1))
            high, low = parted(jnp.concatenate(stack, axis=0))
            spec = dot(high, turn_hi[...]) + dot(low, turn_hi[...]) + dot(high, turn_lo[...])
            count = groups * ROWS
            normed, grads, taps, short, medium = [
                (spec[i * count : (i + 1) * count, :LANES], spec[i * count : (i + 1) * count, LANES:])
                for i in range(5)
            ]
            shorted = times(short, normed)
            grad_long = times_conj(grads, times(medium, shorted))
            grad_filtered = times_conj(grads, taps)
            grad_medium = times_conj(grad_filtered, shorted)
            grad_shorted = times_conj(grad_filtered, medium)
            grad_short = times_conj(grad_shorted, normed)
            grad_normed = times_conj(grad_shorted, short)
            stack = [
                jnp.concatenate(value, axis=1)
                for value in (grad_normed, grad_long, grad_medium, grad_short)
            ]
            high, low = parted(jnp.concatenate(stack, axis=0))
            step = (
                dot(high, turn_back_hi[...])
                + dot(low, turn_back_hi[...])
                + dot(high, turn_back_lo[...])
            )
            for signal in range(2):
                for group in range(groups):
                    at = signal * count + group * ROWS
                    lanes = slice(group * LANES, (group + 1) * LANES)
                    value = (step[at : at + ROWS, :LANES], step[at : at + ROWS, LANES:])
                    turned = times_conj(value, (t_re, t_im))
                    for where, part in zip((top, bottom), turned):
                        part_hi, part_lo = parted(part)
                        last_hi[signal, pl.ds(where, ROWS), lanes] = part_hi
                        last_lo[signal, pl.ds(where, ROWS), lanes] = part_lo
            result = []
            for signal in range(2):
                for group in range(groups):
                    at = (2 + signal) * count + group * ROWS
                    real = step[at : at + ROWS, :LANES] * t_re + step[at : at + ROWS, LANES:] * t_im
                    result.append(sums[signal * groups + group] + real)
            return tuple(result)

        zero = jnp.zeros((ROWS, LANES), jnp.float32)
        sums = lax.fori_loop(0, outer, at_freq, (zero,) * (2 * groups))
        for signal in range(2):
            value = (
                dot(back_hi[...], last_hi[signal])
                + dot(back_hi[...], last_lo[signal])
                + dot(back_lo[...], last_hi[signal])
            )
            for group in range(groups):
                rows = rows_at(local, group)
                for block in range(blocks):
                    part = value[
                        block * ROWS : (block + 1) * ROWS, group * LANES : (group + 1) * LANES
                    ]
                    lanes = slice((block % per) * LANES, (block % per + 1) * LANES)
                    if signal == 0:
                        leaving[block // per, rows, lanes] = (part * scale).astype(jnp.bfloat16)
                    else:
                        long_out[rows, block * LANES : (block + 1) * LANES] = part * (scale * root)
            if signal == 0:
                each_partner(lambda d: outward(chunk, d).start())
        for group in range(groups):
            rows = rows_at(local, group)
            medium_out[rows, :] = sums[group] * (scale * root)
            short_out[rows, :] = sums[groups + group] * (scale * root)

    lax.fori_loop(0, chunks, work, None)
    normed_out[my_rows, :] = leaving[me]

    def finish(chunk, none):
        def one(d):
            inward(0, chunk, d).wait_send()
            inward(1, chunk, d).wait_send()
            outward(chunk, d).wait()

        each_partner(one)

    lax.fori_loop(0, chunks, finish, None)


def on_device(block_input, norm_gain, short_taps, medium_taps, long_filter, grad_out):
    chans, tokens = block_input.shape
    seq_count = lax.axis_size("seq")
    ch_count = lax.axis_size("ch")
    group = chans // seq_count
    length = seq_count * tokens
    short_count = short_taps.shape[1]
    blocks = length // LANES
    outer = blocks + 1
    size = min(group, SIZE if blocks <= 16 else ROWS)
    chunks = group // size
    offset = lax.axis_index("seq") * group
    short = lax.dynamic_slice_in_dim(short_taps, offset, group, 0)
    short = jnp.pad(short, ((0, 0), (0, LANES - short_count)))
    consts = [jnp.asarray(t) for t in tables(blocks)]
    vmem = pl.BlockSpec(memory_space=pltpu.VMEM)
    lanes = size // ROWS * LANES
    normed, long, med, sho = pl.pallas_call(
        functools.partial(fused_kernel, blocks, size, chunks, chans * ch_count),
        in_specs=[vmem] * (6 + len(consts)),
        out_specs=[vmem] * 4,
        out_shape=[
            jax.ShapeDtypeStruct((chans, tokens), jnp.bfloat16),
            jax.ShapeDtypeStruct((group, length), jnp.float32),
            jax.ShapeDtypeStruct((group, LANES), jnp.float32),
            jax.ShapeDtypeStruct((group, LANES), jnp.float32),
        ],
        scratch_shapes=[
            pltpu.VMEM((chans, tokens), jnp.bfloat16),
            pltpu.VMEM((seq_count, group, tokens), jnp.bfloat16),
            pltpu.VMEM((seq_count, group, tokens), jnp.bfloat16),
            pltpu.VMEM((seq_count, group, tokens), jnp.bfloat16),
            pltpu.VMEM((ch_count, 8, tokens), jnp.float32),
            pltpu.VMEM((3, 2 * outer * ROWS, lanes), jnp.float32),
            pltpu.VMEM((2, 2 * outer * ROWS, lanes), jnp.bfloat16),
            pltpu.VMEM((2, 2 * outer * ROWS, lanes), jnp.bfloat16),
            pltpu.SemaphoreType.DMA((3, chunks, seq_count)),
            pltpu.SemaphoreType.DMA((3, chunks, seq_count)),
            pltpu.SemaphoreType.DMA((ch_count,)),
            pltpu.SemaphoreType.DMA((ch_count,)),
        ],
        compiler_params=pltpu.CompilerParams(
            vmem_limit_bytes=58 * 1024 * 1024, collective_id=0, has_side_effects=True
        ),
    )(block_input, grad_out, long_filter, norm_gain[:, None], short, medium_taps, *consts)
    return (normed, long, med[:, : medium_taps.shape[1]], sho[:, :short_count])


def solution(mesh):
    placed = (
        P("ch", "seq"),
        P("ch"),
        P("ch", None),
        P("ch", None),
        P(("ch", "seq"), None),
        P("ch", "seq"),
    )
    return jax.shard_map(
        on_device,
        mesh=mesh,
        in_specs=placed,
        out_specs=(
            P("ch", "seq"),
            P(("ch", "seq"), None),
            P(("ch", "seq"), None),
            P(("ch", "seq"), None),
        ),
        check_vma=False,
    )
```

```python
import functools
import math

import jax
import jax.numpy as jnp
import ml_dtypes
import numpy as np
from jax import lax
from jax.experimental import pallas as pl
from jax.experimental.pallas import tpu as pltpu
from jax.sharding import PartitionSpec as P

LANES = 128
ROWS = 16
SIZE = 64
FREQS = 4


def halves(table):
    high = table.astype(np.float32).astype(ml_dtypes.bfloat16)
    low = (table - high.astype(np.float64)).astype(np.float32).astype(ml_dtypes.bfloat16)
    return high, low


@functools.lru_cache(maxsize=None)
def tables(blocks):
    outer = blocks + 1
    k = np.arange(outer)[:, None]
    a = np.arange(blocks)[None, :]
    q = np.arange(LANES)
    angle = 2.0 * math.pi * ((4 * k + 1) * a % (4 * outer)) / (4.0 * outer)
    eye = np.eye(ROWS)
    split = np.stack([np.cos(angle), -np.sin(angle)])
    ahead = np.einsum("xka,cd->xkcad", split, eye)
    ahead = ahead.reshape(2 * outer * ROWS, blocks * ROWS)
    back = ahead.T
    twist = 2.0 * math.pi * (4 * k + 1) * q[None, :] / (4.0 * outer * LANES)
    twist_re = np.repeat(np.cos(twist), ROWS, axis=0).astype(np.float32)
    twist_im = np.repeat(-np.sin(twist), ROWS, axis=0).astype(np.float32)
    inner = 2.0 * math.pi * (q[:, None] * q[None, :] % LANES) / LANES
    cos, sin = np.cos(inner), np.sin(inner)
    turn = np.block([[cos, -sin], [sin, cos]])
    return (
        *halves(ahead),
        halves(back)[0],
        twist_re,
        twist_im,
        *halves(turn),
        halves(turn.T)[0],
    )


def times(a, b):
    return (a[0] * b[0] - a[1] * b[1], a[0] * b[1] + a[1] * b[0])


def times_conj(a, b):
    return (a[0] * b[0] + a[1] * b[1], a[1] * b[0] - a[0] * b[1])


def dot(a, b):
    return jnp.dot(a, b, preferred_element_type=jnp.float32)


def parted(value):
    high = value.astype(jnp.bfloat16)
    return high, (value - high.astype(jnp.float32)).astype(jnp.bfloat16)


def fused_kernel(
    blocks,
    size,
    chunks,
    total_chans,
    x_ref,
    g_ref,
    h_ref,
    gain_ref,
    short_ref,
    medium_ref,
    ahead_hi,
    ahead_lo,
    back_hi,
    twist_re,
    twist_im,
    turn_hi,
    turn_lo,
    turn_back_hi,
    normed_out,
    long_out,
    medium_out,
    short_out,
    gain_rows,
    normed_ref,
    x_in,
    g_in,
    leaving,
    squares,
    h_in,
    first,
    last_hi,
    last_lo,
    send_sem,
    recv_sem,
    square_send,
    square_recv,
    fetch_sem,
):
    seq_count, group_chans, tokens = x_in.shape
    ch_count = squares.shape[0]
    me = lax.axis_index("seq")
    my_ch = lax.axis_index("ch")
    outer = blocks + 1
    groups = size // ROWS
    per = tokens // LANES
    half = outer * ROWS
    scale = 1.0 / (outer * LANES)
    root = (blocks * LANES) ** (-0.5)

    barrier = pltpu.get_barrier_semaphore()
    for d in range(1, seq_count):
        pl.semaphore_signal(
            barrier,
            inc=1,
            device_id={"seq": lax.rem(me + d, seq_count)},
            device_id_type=pl.DeviceIdType.MESH,
        )
    for d in range(1, ch_count):
        pl.semaphore_signal(
            barrier,
            inc=1,
            device_id={"ch": lax.rem(my_ch + d, ch_count)},
            device_id_type=pl.DeviceIdType.MESH,
        )
    pl.semaphore_wait(barrier, seq_count + ch_count - 2)

    def aligned(row):
        return pl.multiple_of(row, ROWS)

    def inward(which, chunk, d):
        to = lax.rem(me + d, seq_count)
        source = (g_ref, normed_ref)[which]
        target = (g_in, x_in)[which]
        return pltpu.make_async_remote_copy(
            src_ref=source.at[pl.ds(aligned(to * group_chans + chunk * size), size)],
            dst_ref=target.at[me, pl.ds(aligned(chunk * size), size)],
            send_sem=send_sem.at[which, chunk, d],
            recv_sem=recv_sem.at[which, chunk, d],
            device_id={"seq": to},
            device_id_type=pl.DeviceIdType.MESH,
        )

    def outward(chunk, d):
        to = lax.rem(me + d, seq_count)
        return pltpu.make_async_remote_copy(
            src_ref=leaving.at[to, pl.ds(aligned(chunk * size), size)],
            dst_ref=normed_out.at[pl.ds(aligned(me * group_chans + chunk * size), size)],
            send_sem=send_sem.at[2, chunk, d],
            recv_sem=recv_sem.at[2, chunk, d],
            device_id={"seq": to},
            device_id_type=pl.DeviceIdType.MESH,
        )

    def square_copy(d):
        return pltpu.make_async_remote_copy(
            src_ref=squares.at[my_ch],
            dst_ref=squares.at[my_ch],
            send_sem=square_send.at[d],
            recv_sem=square_recv.at[d],
            device_id={"ch": lax.rem(my_ch + d, ch_count)},
            device_id_type=pl.DeviceIdType.MESH,
        )

    def each_partner(act):
        lax.fori_loop(1, seq_count, lambda d, none: act(d), None)

    each_partner(lambda d: inward(0, 0, d).start())
    fetch = pltpu.make_async_copy(h_ref, h_in, fetch_sem)
    fetch.start()
    my_rows = pl.ds(aligned(me * group_chans), group_chans)
    g_in[me] = g_ref[my_rows, :]

    step = 8 * ROWS

    def add_rows(i, total):
        value = x_ref[pl.ds(aligned(i * step), step), :].astype(jnp.float32)
        return total + jnp.sum((value * value).reshape(step // 8, 8, tokens), axis=0)

    squares[my_ch] = lax.fori_loop(
        0, x_ref.shape[0] // step, add_rows, jnp.zeros((8, tokens), jnp.float32)
    )
    for d in range(1, ch_count):
        square_copy(d).start()

    def spread(i, none):
        wide = jnp.broadcast_to(gain_ref[pl.ds(i, 1), :], (LANES, LANES))
        gain_rows[pl.ds(aligned(i * LANES), LANES), :] = wide.T

    lax.fori_loop(0, gain_ref.shape[0], spread, None)
    for d in range(1, ch_count):
        square_copy(d).wait()
    mean = jnp.sum(jnp.sum(squares[...], axis=0), axis=0, keepdims=True) / total_chans
    inv_rms = lax.rsqrt(mean + 1e-05)

    def prepare(chunk, none):
        def one(d, none):
            to = lax.rem(me + d, seq_count)
            at = pl.ds(aligned(to * group_chans + chunk * size), size)
            gain = jnp.concatenate([gain_rows[at, :]] * per, axis=1)
            value = x_ref[at, :].astype(jnp.float32) * inv_rms * gain
            normed_ref[at, :] = value.astype(jnp.bfloat16)

            @pl.when(d > 0)
            def _():
                inward(1, chunk, d).start()

        lax.fori_loop(0, seq_count, one, None)

        @pl.when(chunk + 1 < chunks)
        def _():
            each_partner(lambda d: inward(0, chunk + 1, d).start())

    lax.fori_loop(0, chunks, prepare, None)
    x_in[me] = normed_ref[my_rows, :]
    fetch.wait()

    def work(chunk, none):
        def arrive(d):
            inward(0, chunk, d).wait_recv()
            inward(1, chunk, d).wait_recv()

        each_partner(arrive)
        local = chunk * size
        mine = me * group_chans + local

        def rows_at(start, group):
            return pl.ds(aligned(start + group * ROWS), ROWS)

        def piece(ref, group, block):
            lanes = slice((block % per) * LANES, (block % per + 1) * LANES)
            return ref[block // per, rows_at(local, group), lanes]

        for group in range(groups):
            lanes = slice(group * LANES, (group + 1) * LANES)
            rows = rows_at(local, group)
            normed = jnp.concatenate([piece(x_in, group, b) for b in range(blocks)], axis=0)
            grads = jnp.concatenate([piece(g_in, group, b) for b in range(blocks)], axis=0)
            taps = jnp.concatenate(
                [h_in[rows, b * LANES : (b + 1) * LANES] for b in range(blocks)], axis=0
            )
            taps_hi, taps_lo = parted(taps)
            pair = jnp.concatenate([normed, grads], axis=1)
            both = dot(ahead_hi[...], pair) + dot(ahead_lo[...], pair)
            first[0, :, lanes] = both[:, :LANES]
            first[1, :, lanes] = both[:, LANES:]
            pair = jnp.concatenate([taps_hi, taps_lo], axis=1)
            both = dot(ahead_hi[...], pair)
            first[2, :, lanes] = both[:, :LANES] + both[:, LANES:] + dot(ahead_lo[...], taps_hi)

        def at_freqs(start, width, sums):
            stack = []
            places = []
            for k in range(width):
                top = aligned((start + k) * ROWS)
                bottom = aligned(half + (start + k) * ROWS)
                t_re = twist_re[pl.ds(top, ROWS), :]
                t_im = twist_im[pl.ds(top, ROWS), :]
                places.append((top, bottom, t_re, t_im))
                for signal in range(3):
                    for group in range(groups):
                        lanes = slice(group * LANES, (group + 1) * LANES)
                        value = (
                            first[signal, pl.ds(top, ROWS), lanes],
                            first[signal, pl.ds(bottom, ROWS), lanes],
                        )
                        stack.append(jnp.concatenate(times(value, (t_re, t_im)), axis=1))
                for ref, begin in ((short_ref, local), (medium_ref, mine)):
                    for group in range(groups):
                        taps = ref[rows_at(begin, group), :].astype(jnp.float32)
                        stack.append(jnp.concatenate([taps * t_re, taps * t_im], axis=1))
            high, low = parted(jnp.concatenate(stack, axis=0))
            spec = dot(high, turn_hi[...]) + dot(low, turn_hi[...]) + dot(high, turn_lo[...])
            count = groups * ROWS
            stack = []
            for k in range(width):
                normed, grads, taps, short, medium = [
                    (spec[i * count : (i + 1) * count, :LANES], spec[i * count : (i + 1) * count, LANES:])
                    for i in range(5 * k, 5 * k + 5)
                ]
                shorted = times(short, normed)
                grad_long = times_conj(grads, times(medium, shorted))
                grad_filtered = times_conj(grads, taps)
                grad_medium = times_conj(grad_filtered, shorted)
                grad_shorted = times_conj(grad_filtered, medium)
                grad_short = times_conj(grad_shorted, normed)
                grad_normed = times_conj(grad_shorted, short)
                stack += [
                    jnp.concatenate(value, axis=1)
                    for value in (grad_normed, grad_long, grad_medium, grad_short)
                ]
            high, low = parted(jnp.concatenate(stack, axis=0))
            step = (
                dot(high, turn_back_hi[...])
                + dot(low, turn_back_hi[...])
            )
            sums = list(sums)
            for k, (top, bottom, t_re, t_im) in enumerate(places):
                for signal in range(4):
                    for group in range(groups):
                        at = (4 * k + signal) * count + group * ROWS
                        value = (step[at : at + ROWS, :LANES], step[at : at + ROWS, LANES:])
                        if signal >= 2:
                            real = value[0] * t_re + value[1] * t_im
                            sums[(signal - 2) * groups + group] += real
                            continue
                        lanes = slice(group * LANES, (group + 1) * LANES)
                        turned = times_conj(value, (t_re, t_im))
                        for where, part in zip((top, bottom), turned):
                            part_hi, part_lo = parted(part)
                            last_hi[signal, pl.ds(where, ROWS), lanes] = part_hi
                            last_lo[signal, pl.ds(where, ROWS), lanes] = part_lo
            return tuple(sums)

        zero = jnp.zeros((ROWS, LANES), jnp.float32)
        sums = at_freqs(0, 1, (zero,) * (2 * groups))
        sums = lax.fori_loop(
            0, blocks // FREQS, lambda i, s: at_freqs(1 + i * FREQS, FREQS, s), sums
        )
        for signal in range(2):
            value = (
                dot(back_hi[...], last_hi[signal])
                + dot(back_hi[...], last_lo[signal])
            )
            for group in range(groups):
                rows = rows_at(local, group)
                for block in range(blocks):
                    part = value[
                        block * ROWS : (block + 1) * ROWS, group * LANES : (group + 1) * LANES
                    ]
                    lanes = slice((block % per) * LANES, (block % per + 1) * LANES)
                    if signal == 0:
                        leaving[block // per, rows, lanes] = (part * scale).astype(jnp.bfloat16)
                    else:
                        long_out[rows, block * LANES : (block + 1) * LANES] = part * (scale * root)
            if signal == 0:
                each_partner(lambda d: outward(chunk, d).start())
        for group in range(groups):
            rows = rows_at(local, group)
            medium_out[rows, :] = sums[group] * (scale * root)
            short_out[rows, :] = sums[groups + group] * (scale * root)

    lax.fori_loop(0, chunks, work, None)
    normed_out[my_rows, :] = leaving[me]

    def finish(chunk, none):
        def one(d):
            inward(0, chunk, d).wait_send()
            inward(1, chunk, d).wait_send()
            outward(chunk, d).wait()

        each_partner(one)

    lax.fori_loop(0, chunks, finish, None)


def on_device(block_input, norm_gain, short_taps, medium_taps, long_filter, grad_out):
    chans, tokens = block_input.shape
    seq_count = lax.axis_size("seq")
    ch_count = lax.axis_size("ch")
    group = chans // seq_count
    length = seq_count * tokens
    short_count = short_taps.shape[1]
    blocks = length // LANES
    outer = blocks + 1
    size = min(group, SIZE if blocks <= 16 else ROWS)
    chunks = group // size
    offset = lax.axis_index("seq") * group
    short = lax.dynamic_slice_in_dim(short_taps, offset, group, 0)
    short = jnp.pad(short, ((0, 0), (0, LANES - short_count)))
    consts = [jnp.asarray(t) for t in tables(blocks)]
    vmem = pl.BlockSpec(memory_space=pltpu.VMEM)
    lanes = size // ROWS * LANES
    normed, long, med, sho = pl.pallas_call(
        functools.partial(fused_kernel, blocks, size, chunks, chans * ch_count),
        in_specs=[vmem] * 2 + [pl.BlockSpec(memory_space=pl.ANY)] + [vmem] * (3 + len(consts)),
        out_specs=[vmem] * 4,
        out_shape=[
            jax.ShapeDtypeStruct((chans, tokens), jnp.bfloat16),
            jax.ShapeDtypeStruct((group, length), jnp.float32),
            jax.ShapeDtypeStruct((group, LANES), jnp.float32),
            jax.ShapeDtypeStruct((group, LANES), jnp.float32),
        ],
        scratch_shapes=[
            pltpu.VMEM((chans, LANES), jnp.float32),
            pltpu.VMEM((chans, tokens), jnp.bfloat16),
            pltpu.VMEM((seq_count, group, tokens), jnp.bfloat16),
            pltpu.VMEM((seq_count, group, tokens), jnp.bfloat16),
            pltpu.VMEM((seq_count, group, tokens), jnp.bfloat16),
            pltpu.VMEM((ch_count, 8, tokens), jnp.float32),
            pltpu.VMEM((group, length), jnp.float32),
            pltpu.VMEM((3, 2 * outer * ROWS, lanes), jnp.float32),
            pltpu.VMEM((2, 2 * outer * ROWS, lanes), jnp.bfloat16),
            pltpu.VMEM((2, 2 * outer * ROWS, lanes), jnp.bfloat16),
            pltpu.SemaphoreType.DMA((3, chunks, seq_count)),
            pltpu.SemaphoreType.DMA((3, chunks, seq_count)),
            pltpu.SemaphoreType.DMA((ch_count,)),
            pltpu.SemaphoreType.DMA((ch_count,)),
            pltpu.SemaphoreType.DMA,
        ],
        compiler_params=pltpu.CompilerParams(
            vmem_limit_bytes=58 * 1024 * 1024, collective_id=0, has_side_effects=True
        ),
    )(block_input, grad_out, long_filter, norm_gain.reshape(-1, LANES), short, medium_taps, *consts)
    return (normed, long, med[:, : medium_taps.shape[1]], sho[:, :short_count])


def solution(mesh):
    placed = (
        P("ch", "seq"),
        P("ch"),
        P("ch", None),
        P("ch", None),
        P(("ch", "seq"), None),
        P("ch", "seq"),
    )
    return jax.shard_map(
        on_device,
        mesh=mesh,
        in_specs=placed,
        out_specs=(
            P("ch", "seq"),
            P(("ch", "seq"), None),
            P(("ch", "seq"), None),
            P(("ch", "seq"), None),
        ),
        check_vma=False,
    )
```
